256 devices in a mesh: ctx: 16 (over y, x_hi, core), head: 16 (over z, x_lo).
Axes of the slice: x: 4 (x_hi: 2, x_lo: 2; x = x_hi * 2 + x_lo), y: 4, z: 8, core: 2. Of those that a mesh axis runs over, the one named last changes fastest.
Arguments:
- queries: bfloat16 [2048, 24576], P('ctx', 'head'), may hold values from -8 to 8
- kv_latent: bfloat16 [2048, 576], P('ctx'), may hold values from -7 to 7
- w_uk: bfloat16 [128, 512, 128], P('head'), may hold values from -0.25 to 0.25
- w_uv: bfloat16 [128, 512, 128], P('head'), may hold values from -0.25 to 0.25
- w_out: bfloat16 [16384, 7168], P('head', 'ctx'), may hold values from -0.046875 to 0.046875
- doc_lengths: int32 [8], replicated, may hold values from 1 to 1152, 2048 in all
Outputs:
- attn_out: bfloat16 [2048, 7168], P('ctx', 'head')
The draws below stay inside these ranges and needn't reach their ends.
Inputs may be any that keep to these rules, and one draw needn't show every extreme that they name: `doc_lengths`: the lengths sum to 2048.
All inputs are finite; a program needn't handle non-finite values.
Results may differ from the reference program's by a relative error of at most 0.028.
Values may be sent and summed in bfloat16 or wider, within the bound.
No kernel may reach another device: no remote copies, remote signals or barrier semaphores. Data moves between devices by JAX's collectives and lax.ppermute only.
A program may use at most 128 MiB of HBM per device.

```python
import math
import jax
import jax.numpy as jnp
import numpy as np
from jax import lax

D = 7168
HEADS = 128
KVL = 512
ROPE = 64
NOPE = 128
VDIM = 128
TOKENS = 2048
DOCS = 8
MOST_DOC = 1152


def draw_kv_latent(key, part):
    key = jax.random.fold_in(key, 11)
    return jnp.clip(jax.random.normal(key, (TOKENS, KVL + ROPE), jnp.float32), -6.0, 6.0).astype(jnp.bfloat16)


def draw_queries(key, part):
    key = jax.random.fold_in(key, 23)
    base = jnp.clip(jax.random.normal(key, (TOKENS, HEADS * (NOPE + ROPE)), jnp.float32), -6.0, 6.0)
    return base.astype(jnp.bfloat16)


def block_levels(stream_key, shape, pieces, smallest, top_value):
    gain = 1.0
    for dim, blocks in pieces:
        draws = jax.random.uniform(jax.random.fold_in(jax.random.fold_in(stream_key, 6), dim), (blocks,), jnp.float32, smallest / len(pieces), top_value / len(pieces))
        gain = gain * jnp.repeat(jnp.exp(draws), shape[dim] // blocks).reshape((-1,) + (1,) * (len(shape) - 1 - dim))
    return gain


def split_up(amount, total, most, lean):
    weights = [(1 << 20) // math.isqrt(grade ** lean) + 1 for grade in range(2, amount + 1)]
    spare, holding = total - most - (amount - 1), [1] * (amount - 1)
    while spare > 0:
        movable = [i for i in range(amount - 1) if holding[i] < most]
        pool, remaining = sum([weights[i] for i in movable]), spare
        for i in movable:
            addition = min(most - holding[i], max(1, remaining * weights[i] // pool), spare)
            holding[i] = holding[i] + addition
            spare = spare - addition
    return np.array([most] + holding)


def ragged(rng, number_of, total, bound, slope):
    if number_of == 2:
        one = jax.random.randint(rng, (), max(1, total - bound), min(bound, total - 1) + 1)
        return jnp.stack([one, total - one])
    lengths = jnp.asarray(split_up(number_of, total, bound, slope), jnp.int32)
    pairs = (number_of - 1) // 2
    source_of, receiver = lengths[1:1 + 2 * pairs:2], lengths[2:2 + 2 * pairs:2]
    slack = jnp.minimum(source_of - 1, bound - receiver)
    moved = jax.random.randint(jax.random.fold_in(rng, 1), (pairs,), 0, 1 << 20) % (slack + 1)
    lengths = lengths.at[1:1 + 2 * pairs:2].set(source_of - moved).at[2:2 + 2 * pairs:2].set(receiver + moved)
    return lengths[jax.random.permutation(jax.random.fold_in(rng, 2), number_of)]


def scatter_about(stream_key, extent, spread, reach, cuts=(), kind=jnp.bfloat16):
    factor_of = block_levels(stream_key, extent, cuts, -0.22, 0.18) if cuts else 1.0
    array = jax.random.normal(stream_key, extent, jnp.float32) * spread * factor_of
    return jnp.minimum(jnp.maximum(array, -reach), reach).astype(kind)


def setup_inputs(seed: int = 0) -> dict:
    key_of = jax.random.split(jax.random.key(seed), 7)
    return {
        "queries": draw_queries(jax.random.fold_in(key_of[6], 71), 0),
        "kv_latent": draw_kv_latent(jax.random.fold_in(key_of[6], 71), 0),
        "w_uk": scatter_about(key_of[2], (HEADS, KVL, NOPE), KVL ** -0.5, 0.25, ((0, 16),)),
        "w_uv": scatter_about(key_of[3], (HEADS, KVL, VDIM), KVL ** -0.5, 0.25, ((0, 16),)),
        "w_out": scatter_about(key_of[4], (HEADS * VDIM, D), (HEADS * VDIM) ** -0.5, 0.046875, ((0, 16), (1, 16))),
        "doc_lengths": ragged(key_of[5], DOCS, TOKENS, MOST_DOC, 2).astype(jnp.int32),
    }


def doc_index(positions, doc_lengths):
    ends = jnp.cumsum(doc_lengths).astype(jnp.int32)
    return lax.optimization_barrier(jnp.sum((positions[:, None] >= ends[None, :]).astype(jnp.int32), axis=1))

def reference(queries, kv_latent, w_uk, w_uv, w_out, doc_lengths):
    positions = jnp.arange(TOKENS, dtype=jnp.int32)
    docs = doc_index(positions, doc_lengths)
    visible = (positions[None, :] <= positions[:, None]) & (docs[None, :] == docs[:, None])
    per_head = queries.reshape(TOKENS, HEADS, NOPE + ROPE).transpose(1, 0, 2)
    score_scale = 1.0 / math.sqrt(NOPE + ROPE)
    latents = kv_latent[:, :KVL]

    def one_head(operands):
        query, key_map, value_map = operands
        absorbed = jnp.dot(query[:, :NOPE], key_map.T, preferred_element_type=jnp.float32).astype(jnp.bfloat16)
        joined = jnp.concatenate([absorbed, query[:, NOPE:]], axis=1)
        scores = jnp.dot(joined, kv_latent.T, preferred_element_type=jnp.float32) * score_scale
        scores = jnp.where(visible, scores, -jnp.inf)
        weights = jax.nn.softmax(scores, axis=1).astype(jnp.bfloat16)
        context = jnp.dot(weights, latents, preferred_element_type=jnp.float32).astype(jnp.bfloat16)
        return jnp.dot(context, value_map, preferred_element_type=jnp.float32).astype(jnp.bfloat16)
    outputs = lax.map(one_head, (per_head, w_uk, w_uv))
    flat = outputs.transpose(1, 0, 2).reshape(TOKENS, HEADS * VDIM)
    return jnp.dot(flat, w_out, preferred_element_type=jnp.float32).astype(jnp.bfloat16)
```

```python
import functools
import math

import jax
import jax.numpy as jnp
from jax import lax
from jax.experimental import pallas as pl
from jax.experimental.pallas import tpu as pltpu
from jax.sharding import PartitionSpec as P

AXES = ("ctx", "head")
VMEM = pltpu.MemorySpace.VMEM
SMEM = pltpu.MemorySpace.SMEM
NEVER = -1e30


def index_of(y, xh, core, z, xl):
    return ((y * 2 + xh) * 2 + core) * 16 + z * 2 + xl


PLACES = [
    (y, xh, core, z, xl)
    for y in range(4)
    for xh in range(2)
    for core in range(2)
    for z in range(8)
    for xl in range(2)
]


def send(value, target):
    pairs = []
    for place in PLACES:
        goal = target(*place)
        if goal is not None:
            pairs.append((index_of(*place), index_of(*goal)))
    return lax.ppermute(value, AXES, pairs)


def other_core(y, xh, core, z, xl):
    return (y, xh, 1 - core, z, xl)


def other_lo(y, xh, core, z, xl):
    return (y, xh, core, z, 1 - xl)


def absorb_kernel(q_ref, w_uk_ref, qc_ref, qr_ref):
    heads, rows = w_uk_ref.shape[0], q_ref.shape[0]
    for h in range(heads):
        nope = q_ref[:, h * 192 : h * 192 + 128]
        qc_ref[h * rows : (h + 1) * rows, :] = lax.dot_general(
            nope, w_uk_ref[h], (((1,), (1,)), ((), ())), preferred_element_type=jnp.float32
        ).astype(jnp.bfloat16)
        qr_ref[h * rows : (h + 1) * rows, :] = q_ref[:, h * 192 + 128 : (h + 1) * 192]


def attend_kernel(info_ref, qc_ref, qr_ref, w_uv_ref, *rest):
    units = (len(rest) - 5) // 2
    blocks = rest[: 2 * units]
    out_ref, kv_ref, scores_ref, accum_ref, sems = rest[2 * units :]
    rows, latent = qc_ref.shape
    heads = w_uv_ref.shape[0]
    tokens = rows // heads
    query_base = info_ref[8]
    copies = []
    for u in range(units):
        for half in range(2):
            copies.append(
                pltpu.make_async_copy(
                    blocks[2 * u + half],
                    kv_ref.at[u, :, pl.ds(half * 128, 128)],
                    sems.at[2 * u + half],
                )
            )
    for copy in copies:
        copy.start()
    query_pos = query_base + lax.broadcasted_iota(jnp.int32, (tokens, 1), 0)
    start = jnp.zeros((tokens, 1), jnp.int32)
    first = jnp.int32(0)
    end = jnp.int32(0)
    for k in range(8):
        end = end + info_ref[k]
        start = jnp.where(query_pos >= end, end, start)
        first = jnp.where(query_base >= end, end, first)
    for copy in copies:
        copy.wait()
    lane = lax.broadcasted_iota(jnp.int32, (1, 256), 1)
    scale = 1.0 / math.sqrt(192.0) * math.log2(math.e)

    def seen(u):
        base = info_ref[16 + u]
        return (base <= query_base + tokens - 1) & (base + 256 > first)

    def base_of(u):
        return info_ref[16 + u], info_ref[32 + u]

    def look(u, highest):
        def yes():
            base, flip = base_of(u)
            key_pos = base + jnp.where(flip > 0, lax.rem(lane + 128, 256), lane)
            visible = (key_pos <= query_pos) & (key_pos >= start)
            s = jnp.dot(qc_ref[...], kv_ref[u, :latent, :], preferred_element_type=jnp.float32)
            s = s + jnp.dot(qr_ref[...], kv_ref[u, latent:, :], preferred_element_type=jnp.float32)
            s = jnp.where(visible[None], s.reshape(heads, tokens, 256), NEVER)
            scores_ref[u] = s.reshape(rows, 256)
            top = jnp.maximum(s[:, :, :128], s[:, :, 128:]).reshape(rows, 128)
            return jnp.maximum(highest, top)

        return lax.cond(seen(u), yes, lambda: highest)

    highest = lax.fori_loop(0, units, look, jnp.full((rows, 128), NEVER, jnp.float32))
    peak = jnp.max(highest, axis=1, keepdims=True) * scale
    accum_ref[...] = jnp.zeros_like(accum_ref)

    def gather(u, total):
        def yes():
            p = jnp.exp2(scores_ref[u] * scale - peak)
            accum_ref[...] += lax.dot_general(
                p.astype(jnp.bfloat16),
                kv_ref[u, :latent, :],
                (((1,), (1,)), ((), ())),
                preferred_element_type=jnp.float32,
            )
            return total + p[:, :128] + p[:, 128:]

        return lax.cond(seen(u), yes, lambda: total)

    total = lax.fori_loop(0, units, gather, jnp.zeros((rows, 128), jnp.float32))
    inverse = 1.0 / jnp.sum(total, axis=1, keepdims=True)
    for h in range(heads):
        context = (
            accum_ref[h * tokens : (h + 1) * tokens, :] * inverse[h * tokens : (h + 1) * tokens]
        ).astype(jnp.bfloat16)
        out_ref[:, h * 128 : (h + 1) * 128] = jnp.dot(
            context, w_uv_ref[h], preferred_element_type=jnp.float32
        ).astype(jnp.bfloat16)


def whole(space):
    return pl.BlockSpec(memory_space=space)


def body(queries, kv_latent, w_uk, w_uv, w_out, doc_lengths):
    rows = queries.shape[0]
    heads, latent, nope = w_uk.shape
    ctx = lax.axis_index("ctx")
    head = lax.axis_index("head")
    y, xh, core = ctx // 4, (ctx // 2) % 2, ctx % 2
    z, xl = head // 2, head % 2
    width = w_out.shape[1]

    mine = kv_latent.T

    def from_y(step, flip):
        def target(ty, txh, tcore, tz, txl):
            if ty + step > 3:
                return None
            if flip:
                return (ty + step, 1 - txh, tcore, tz, 1 - txl)
            return (ty + step, txh, tcore, tz, txl)

        return target

    got = [mine, send(mine, lambda ty, txh, tcore, tz, txl: (ty, 1 - txh, tcore, tz, 1 - txl))]
    for step in (1, 2):
        got.append(send(mine, from_y(step, False)))
        got.append(send(mine, from_y(step, True)))

    def farthest(ty, txh, tcore, tz, txl):
        if (ty, txh, tcore) == (0, 1, 1):
            return (3, 0, 0, tz, 1 - txl)
        return None

    far = send(mine, farthest)
    theirs = [send(block, other_core) for block in got]
    blocks = []
    bases = []
    for number, (a, b) in enumerate(zip(got, theirs)):
        step, flip = number // 2, number % 2
        blocks.extend([a, b])
        source = y - step
        source_xh = xh if flip == 0 else 1 - xh
        base = jnp.where(source < 0, 1 << 20, source * 512 + source_xh * 256)
        bases.append(base)
    blocks.extend([far, far])
    bases.append(jnp.where((y == 3) & (xh == 0) & (core == 0), 256, 1 << 20))
    units = len(bases)
    flips = [core] * (units - 1) + [0]
    info = jnp.concatenate(
        [
            doc_lengths,
            jnp.stack([ctx * rows] + [0] * 7).astype(jnp.int32),
            jnp.stack(bases + [0] * (16 - units)).astype(jnp.int32),
            jnp.stack(flips + [0] * (16 - units)).astype(jnp.int32),
        ]
    )

    w_own = w_out.T
    w_got = []
    for s in range(2):

        def target(ty, a, c, tz, xx, s=s):
            return (ty, xx ^ s, a, tz, c)

        w_got.append(send(w_own, target))
    w_theirs = [send(block, other_core) for block in w_got]

    qc, qr = pl.pallas_call(
        absorb_kernel,
        out_shape=(
            jax.ShapeDtypeStruct((heads * rows, latent), jnp.bfloat16),
            jax.ShapeDtypeStruct((heads * rows, 64), jnp.bfloat16),
        ),
        in_specs=[whole(VMEM), whole(VMEM)],
        out_specs=(whole(VMEM), whole(VMEM)),
        compiler_params=pltpu.CompilerParams(vmem_limit_bytes=32 << 20),
        name="absorb",
    )(queries, w_uk)

    values = pl.pallas_call(
        attend_kernel,
        out_shape=jax.ShapeDtypeStruct((rows, heads * 128), jnp.bfloat16),
        in_specs=[whole(SMEM)] + [whole(VMEM)] * 3 + [whole(pl.ANY)] * (2 * units),
        out_specs=whole(VMEM),
        scratch_shapes=[
            pltpu.VMEM((units, latent + 64, 256), jnp.bfloat16),
            pltpu.VMEM((units, heads * rows, 256), jnp.float32),
            pltpu.VMEM((heads * rows, latent), jnp.float32),
            pltpu.SemaphoreType.DMA((2 * units,)),
        ],
        compiler_params=pltpu.CompilerParams(vmem_limit_bytes=48 << 20),
        name="attend",
    )(info, qc, qr, w_uv, *blocks)

    def shifted(step):
        return lambda ty, txh, tcore, tz, txl: ((ty + step) % 4, txh, tcore, tz, txl)

    near = [values] + [send(values, shifted(step)) for step in (1, 2, 3)]
    across = [send(block, other_lo) for block in near]
    own_x = jnp.concatenate(near, axis=0)
    other_x = jnp.concatenate(across, axis=0)
    same = (xh ^ xl) == 0
    x0 = jnp.where(same, own_x, other_x)
    x1 = jnp.where(same, other_x, own_x)

    def times(w0, w1):
        dims = (((1,), (1,)), ((), ()))
        return lax.dot_general(
            x0, w0, dims, preferred_element_type=jnp.float32
        ) + lax.dot_general(x1, w1, dims, preferred_element_type=jnp.float32)

    here = times(w_got[0], w_got[1]).astype(jnp.bfloat16)
    there = times(w_theirs[0], w_theirs[1]).astype(jnp.bfloat16)
    first = core == 0
    partial = jnp.concatenate(
        [jnp.where(first, here, there), jnp.where(first, there, here)], axis=1
    )

    half = rows // 2

    def piece(goal):
        b, d = goal // 2, goal % 2
        at = ((y - b) % 4) * rows + d * half
        return lax.dynamic_slice_in_dim(partial, at, half, axis=0)

    total = piece(z).astype(jnp.float32)
    for step in range(1, 8):
        arrived = send(
            piece((z + step) % 8),
            lambda ty, txh, tcore, tz, txl, step=step: (ty, txh, tcore, (tz + step) % 8, txl),
        )
        total = total + arrived.astype(jnp.float32)
    total = total.astype(jnp.bfloat16)

    even = (z % 2) == 0
    left, right = total[:, :width], total[:, width:]
    out = []
    for s in range(2):

        def target(ty, txh, tcore, tz, txl, s=s):
            b, d = tz // 2, tz % 2
            return (b, txh, tcore, 2 * ty + (d ^ s), txl)

        chosen = jnp.where(even, left, right) if s == 0 else jnp.where(even, right, left)
        out.append(send(chosen, target))
    return jnp.where(
        even,
        jnp.concatenate([out[0], out[1]], axis=0),
        jnp.concatenate([out[1], out[0]], axis=0),
    )


def solution(mesh):
    placed = (
        P("ctx", "head"),
        P("ctx", None),
        P("head", None, None),
        P("head", None, None),
        P("head", "ctx"),
        P(),
    )
    return jax.shard_map(
        body, mesh=mesh, in_specs=placed, out_specs=P("ctx", "head"), check_vma=False
    )
```

```python
import math

import jax
import jax.numpy as jnp
from jax import lax
from jax.experimental import pallas as pl
from jax.experimental.pallas import tpu as pltpu
from jax.sharding import PartitionSpec as P

AXES = ("ctx", "head")
VMEM = pltpu.MemorySpace.VMEM
SMEM = pltpu.MemorySpace.SMEM
NEVER = -1e30


def index_of(y, xh, core, z, xl):
    return ((y * 2 + xh) * 2 + core) * 16 + z * 2 + xl


PLACES = [
    (y, xh, core, z, xl)
    for y in range(4)
    for xh in range(2)
    for core in range(2)
    for z in range(8)
    for xl in range(2)
]


def send(value, target):
    pairs = []
    for place in PLACES:
        goal = target(*place)
        if goal is not None:
            pairs.append((index_of(*place), index_of(*goal)))
    return lax.ppermute(value, AXES, pairs)


def other_core(y, xh, core, z, xl):
    return (y, xh, 1 - core, z, xl)


def other_lo(y, xh, core, z, xl):
    return (y, xh, core, z, 1 - xl)


def after(value, earlier):
    return lax.optimization_barrier((value, earlier))[0]


def absorb_kernel(q_ref, w_uk_ref, qc_ref, qr_ref):
    heads, rows = w_uk_ref.shape[0], q_ref.shape[0]
    for h in range(heads):
        nope = q_ref[:, h * 192 : h * 192 + 128]
        qc_ref[h * rows : (h + 1) * rows, :] = lax.dot_general(
            nope, w_uk_ref[h], (((1,), (1,)), ((), ())), preferred_element_type=jnp.float32
        ).astype(jnp.bfloat16)
        qr_ref[h * rows : (h + 1) * rows, :] = q_ref[:, h * 192 + 128 : (h + 1) * 192]


def place_here():
    ctx, head = lax.axis_index("ctx"), lax.axis_index("head")
    return ctx // 4, lax.rem(ctx // 2, 2), lax.rem(ctx, 2), head // 2, lax.rem(head, 2)


def attend_kernel(lengths_ref, qc_ref, qr_ref, w_uv_any, *rest):
    blocks = rest[:13]
    out_ref, kv_ref, scores_ref, accum_ref, highest_ref, total_ref, w_uv_ref, sems = rest[13:]
    y, xh, core, _, _ = place_here()
    rows, latent = qc_ref.shape
    heads = w_uv_ref.shape[0]
    tokens = rows // heads
    units = kv_ref.shape[0]
    query_base = lax.axis_index("ctx") * tokens
    for u in range(units):
        for half in range(2):
            pltpu.make_async_copy(
                blocks[min(2 * u + half, 12)],
                kv_ref.at[u, :, pl.ds(half * 128, 128)],
                sems.at[2 * u + half],
            ).start()
    w_uv_copy = pltpu.make_async_copy(w_uv_any, w_uv_ref, sems.at[2 * units])
    w_uv_copy.start()
    query_pos = query_base + lax.broadcasted_iota(jnp.int32, (tokens, 1), 0)
    start = jnp.zeros((tokens, 1), jnp.int32)
    first = jnp.int32(0)
    end = jnp.int32(0)
    for k in range(8):
        end = end + lengths_ref[k]
        start = jnp.where(query_pos >= end, end, start)
        first = jnp.where(query_base >= end, end, first)
    lane = lax.broadcasted_iota(jnp.int32, (1, 256), 1)
    scale = 1.0 / math.sqrt(192.0) * math.log2(math.e)

    def base_of(u):
        source = y - u // 2
        source_xh = jnp.where(lax.rem(u, 2) == 0, xh, 1 - xh)
        base = jnp.where(source < 0, 1 << 20, source * 512 + source_xh * 256)
        last = jnp.where((y == 3) & (xh == 0) & (core == 0), 256, 1 << 20)
        return jnp.where(u == units - 1, last, base)

    def seen(u):
        base = base_of(u)
        return (base <= query_base + tokens - 1) & (base + 256 > first)

    def look(u, fresh):
        base, flip = base_of(u), jnp.where(u == units - 1, 0, core)
        key_pos = base + jnp.where(flip > 0, lax.rem(lane + 128, 256), lane)
        visible = (key_pos <= query_pos) & (key_pos >= start)
        s = jnp.dot(qc_ref[...], kv_ref[u, :latent, :], preferred_element_type=jnp.float32)
        s = s + jnp.dot(qr_ref[...], kv_ref[u, latent:, :], preferred_element_type=jnp.float32)
        s = jnp.where(visible[None], s.reshape(heads, tokens, 256), NEVER)
        scores_ref[u] = s.reshape(rows, 256)
        top = jnp.maximum(s[:, :, :128], s[:, :, 128:]).reshape(rows, 128)
        highest_ref[...] = top if fresh else jnp.maximum(highest_ref[...], top)

    def wait(u):
        for half in range(2):
            pltpu.make_async_copy(
                blocks[0], kv_ref.at[u, :, pl.ds(half * 128, 128)], sems.at[2 * u + half]
            ).wait()

    wait(0)
    look(0, True)

    @pl.loop(1, units)
    def _(u):
        wait(u)

        @pl.when(seen(u))
        def _():
            look(u, False)

    highest_ref[:, :1] = jnp.max(highest_ref[...], axis=1, keepdims=True) * scale

    def gather(u, fresh):
        p = jnp.exp2(scores_ref[u] * scale - highest_ref[:, :1])
        product = lax.dot_general(
            p.astype(jnp.bfloat16),
            kv_ref[u, :latent, :],
            (((1,), (1,)), ((), ())),
            preferred_element_type=jnp.float32,
        )
        both = p[:, :128] + p[:, 128:]
        accum_ref[...] = product if fresh else accum_ref[...] + product
        total_ref[...] = both if fresh else total_ref[...] + both

    gather(0, True)

    @pl.loop(1, units)
    def _(u):
        @pl.when(seen(u))
        def _():
            gather(u, False)

    w_uv_copy.wait()
    inverse = 1.0 / jnp.sum(total_ref[...], axis=1, keepdims=True)
    for h in range(heads):
        context = (
            accum_ref[h * tokens : (h + 1) * tokens, :] * inverse[h * tokens : (h + 1) * tokens]
        ).astype(jnp.bfloat16)
        out_ref[:, h * 128 : (h + 1) * 128] = jnp.dot(
            context, w_uv_ref[h], preferred_element_type=jnp.float32
        ).astype(jnp.bfloat16)


def project_kernel(*rest):
    sources = rest[:16]
    own_ref, up_ref, down_ref, far_up_ref, far_down_ref, up2_ref, down2_ref = rest[16:23]
    x_ref, w_ref, sems = rest[23:]
    y, xh, core, z, xl = place_here()
    b, d = z // 2, lax.rem(z, 2)

    def x_copy(number):
        part, g = number // 4, number % 4
        at = pl.multiple_of(lax.rem(y - g - b + 8, 4) * 128, 128)
        return pltpu.make_async_copy(
            sources[number],
            x_ref.at[pl.ds(at, 128), pl.ds(part * 1024, 1024)],
            sems.at[number],
        )

    def w_copy(source, order, part):
        return pltpu.make_async_copy(
            source,
            w_ref.at[order, :, pl.ds(part * 1024, 1024)],
            sems.at[8 + 2 * order + part],
        )

    near_order, far_order = lax.rem(xh + d, 2), lax.rem(1 - xh + d, 2)
    kinds = ((near_order, 0), (near_order, 1), (far_order, 1), (far_order, 0))
    for turn in range(2):

        @pl.when(lax.rem(core + xl, 2) == turn)
        def fetch(turn=turn):
            for kind, (order, part) in enumerate(kinds):
                w_copy(sources[8 + 4 * turn + kind], order, part).start()

    for number in range(8):
        x_copy(number).start()
    for number in range(8):
        x_copy(number).wait()
    pieces = []
    for order in range(2):
        for part in range(2):
            w_copy(sources[8], order, part).wait()
        sums = lax.dot_general(
            w_ref[order], x_ref[...], (((1,), (1,)), ((), ())), preferred_element_type=jnp.float32
        ).astype(jnp.bfloat16)
        parts = [sums[:, j * 128 : (j + 1) * 128] for j in range(4)]
        if order == 0:
            own_ref[...], up2_ref[...] = parts[0], parts[1]
            far_up_ref[...], far_down_ref[...] = parts[2][:224], parts[2][224:]
            down2_ref[...] = parts[3]
        else:
            for turn in range(2):

                @pl.when(d == turn)
                def store(turn=turn):
                    for j in range(4):
                        step = (2 * j + 1 - 2 * turn) % 8
                        ref = up_ref if step < 4 else down_ref
                        ref[0 if step in (3, 5) else 1] = parts[j]


def whole(space):
    return pl.BlockSpec(memory_space=space)


def body(queries, kv_latent, w_uk, w_uv, w_out, doc_lengths):
    rows = queries.shape[0]
    heads, latent, nope = w_uk.shape
    width = w_out.shape[1]

    mine = kv_latent.T

    def from_y(step, flip):
        def target(ty, txh, tcore, tz, txl):
            if ty + step > 3:
                return None
            if flip:
                return (ty + step, 1 - txh, tcore, tz, 1 - txl)
            return (ty + step, txh, tcore, tz, txl)

        return target

    def farthest(ty, txh, tcore, tz, txl):
        if (ty, txh, tcore) == (0, 1, 1):
            return (3, 0, 0, tz, 1 - txl)
        return None

    got = [mine, send(mine, from_y(0, True))]
    for step in (1, 2):
        got.extend([send(mine, from_y(step, False)), send(mine, from_y(step, True))])
    far = send(mine, farthest)
    qc, qr = pl.pallas_call(
        absorb_kernel,
        out_shape=(
            jax.ShapeDtypeStruct((heads * rows, latent), jnp.bfloat16),
            jax.ShapeDtypeStruct((heads * rows, 64), jnp.bfloat16),
        ),
        in_specs=[whole(VMEM), whole(VMEM)],
        out_specs=(whole(VMEM), whole(VMEM)),
        compiler_params=pltpu.CompilerParams(vmem_limit_bytes=8 << 20),
        name="absorb",
    )(queries, w_uk)

    blocks = []
    for block in got[:4]:
        blocks.extend([block, send(block, other_core)])
    for block in after(got[4:], (qc, qr)):
        blocks.extend([block, send(block, other_core)])
    blocks.append(far)
    units = len(got) + 1

    def only(test, goal):
        return lambda *at: goal(*at) if test(*at) else None

    def same(ty, h, c, tz, x):
        return c == x

    def differs(ty, h, c, tz, x):
        return c != x

    def around(ty, h, c, tz, x):
        return (ty, 1 - h, 1 - c, tz, x) if c == x else (ty, h, c, tz, 1 - x)

    def across_x(ty, h, c, tz, x):
        return (ty, 1 - h, 1 - c, tz, 1 - x)

    w_own = w_out.T
    w_a = send(w_own, around)
    w_b = send(after(w_own, got), only(differs, across_x))
    w_a_other = send(after(w_a, blocks), other_core)
    w_own_other = send(after(w_own, blocks), only(same, other_core))

    def shifted(step):
        return lambda ty, txh, tcore, tz, txl: ((ty + step) % 4, txh, tcore, tz, txl)

    qc = after(qc, (w_a_other, w_own_other))
    values = pl.pallas_call(
        attend_kernel,
        out_shape=jax.ShapeDtypeStruct((rows, heads * 128), jnp.bfloat16),
        in_specs=[whole(SMEM)] + [whole(VMEM)] * 2 + [whole(pl.ANY)] * 14,
        out_specs=whole(VMEM),
        scratch_shapes=[
            pltpu.VMEM((units, latent + 64, 256), jnp.bfloat16),
            pltpu.VMEM((units, heads * rows, 256), jnp.float32),
            pltpu.VMEM((heads * rows, latent), jnp.float32),
            pltpu.VMEM((heads * rows, 128), jnp.float32),
            pltpu.VMEM((heads * rows, 128), jnp.float32),
            pltpu.VMEM((heads, latent, 128), jnp.bfloat16),
            pltpu.SemaphoreType.DMA((2 * units + 1,)),
        ],
        compiler_params=pltpu.CompilerParams(vmem_limit_bytes=26 << 20),
        name="attend",
    )(doc_lengths, qc, qr, w_uv, *blocks)

    near = [values] + [send(values, shifted(step)) for step in (1, 2, 3)]
    neighbour = send(values, other_lo)
    w_b_other = send(after(w_b, (near, neighbour)), only(differs, other_core))
    w_same = [w_own, w_a, w_b_other, w_a_other]
    w_cross = [w_own_other, w_a_other, w_b, w_a]
    across = [
        neighbour,
        send(neighbour, shifted(1)),
        send(near[2], other_lo),
        send(neighbour, shifted(3)),
    ]

    def result(*shape):
        return jax.ShapeDtypeStruct(shape, jnp.bfloat16)

    own, up, down, far_up, far_down, up2, down2 = pl.pallas_call(
        project_kernel,
        out_shape=[
            result(width, rows),
            result(2, width, rows),
            result(2, width, rows),
            result(width // 2, rows),
            result(width // 2, rows),
            result(width, rows),
            result(width, rows),
        ],
        in_specs=[whole(pl.ANY)] * 16,
        out_specs=[whole(VMEM)] * 7,
        scratch_shapes=[
            pltpu.VMEM((4 * rows, 2048), jnp.bfloat16),
            pltpu.VMEM((2, width, 2048), jnp.bfloat16),
            pltpu.SemaphoreType.DMA((12,)),
        ],
        compiler_params=pltpu.CompilerParams(vmem_limit_bytes=20 << 20),
        name="project",
    )(*near, *across, *w_same, *w_cross)

    def along(step):
        return lambda ty, txh, tcore, tz, txl: (ty, txh, tcore, (tz + step) % 8, txl)

    def wide(value):
        return value.astype(jnp.float32)

    from_far_low = send(far_up, along(2))
    from_far_high = send(far_down, along(6))
    from_low = send(up, along(1))
    from_high = send(down, along(7))
    up_sum = wide(up2) + wide(from_low[0]) + jnp.pad(wide(from_far_low), ((0, width // 2), (0, 0)))
    down_sum = (
        wide(down2) + wide(from_high[0]) + jnp.pad(wide(from_far_high), ((width // 2, 0), (0, 0)))
    )
    total = wide(own) + wide(from_low[1]) + wide(from_high[1])
    total = total + wide(send(up_sum.astype(jnp.bfloat16), along(2)))
    total = total + wide(send(down_sum.astype(jnp.bfloat16), along(6)))
    total = total.astype(jnp.bfloat16)

    def final(ty, txh, tcore, tz, txl):
        return (tz // 2, txh, tcore, 2 * ty + tz % 2, txl)

    return send(total, final).T


def solution(mesh):
    placed = (
        P("ctx", "head"),
        P("ctx", None),
        P("head", None, None),
        P("head", None, None),
        P("head", "ctx"),
        P(),
    )
    return jax.shard_map(
        body, mesh=mesh, in_specs=placed, out_specs=P("ctx", "head"), check_vma=False
    )
```

```python
import math

import jax
import jax.numpy as jnp
from jax import lax
from jax.experimental import pallas as pl
from jax.experimental.pallas import tpu as pltpu
from jax.sharding import PartitionSpec as P

AXES = ("ctx", "head")
VMEM = pltpu.MemorySpace.VMEM
SMEM = pltpu.MemorySpace.SMEM
NEVER = -1e30


def index_of(y, xh, core, z, xl):
    return ((y * 2 + xh) * 2 + core) * 16 + z * 2 + xl


PLACES = [
    (y, xh, core, z, xl)
    for y in range(4)
    for xh in range(2)
    for core in range(2)
    for z in range(8)
    for xl in range(2)
]


def send(value, target):
    pairs = []
    for place in PLACES:
        goal = target(*place)
        if goal is not None:
            pairs.append((index_of(*place), index_of(*goal)))
    return lax.ppermute(value, AXES, pairs)


def other_core(y, xh, core, z, xl):
    return (y, xh, 1 - core, z, xl)


def other_lo(y, xh, core, z, xl):
    return (y, xh, core, z, 1 - xl)


def after(value, earlier):
    return lax.optimization_barrier((value, earlier))[0]


def absorb_kernel(q_ref, w_uk_ref, qc_ref, qr_ref):
    heads, rows = w_uk_ref.shape[0], q_ref.shape[0]
    for h in range(heads):
        nope = q_ref[:, h * 192 : h * 192 + 128]
        qc_ref[h * rows : (h + 1) * rows, :] = lax.dot_general(
            nope, w_uk_ref[h], (((1,), (1,)), ((), ())), preferred_element_type=jnp.float32
        ).astype(jnp.bfloat16)
        qr_ref[h * rows : (h + 1) * rows, :] = q_ref[:, h * 192 + 128 : (h + 1) * 192]


def place_here():
    ctx, head = lax.axis_index("ctx"), lax.axis_index("head")
    return ctx // 4, lax.rem(ctx // 2, 2), lax.rem(ctx, 2), head // 2, lax.rem(head, 2)


def attend_kernel(lengths_ref, qc_ref, qr_ref, w_uv_any, *rest):
    blocks = rest[:13]
    out_ref, kv_ref, scores_ref, accum_ref, highest_ref, total_ref, w_uv_ref, sems = rest[13:]
    y, xh, core, _, _ = place_here()
    rows, latent = qc_ref.shape
    heads = w_uv_ref.shape[0]
    tokens = rows // heads
    units = kv_ref.shape[0]
    query_base = lax.axis_index("ctx") * tokens
    for u in range(units):
        for half in range(2):
            pltpu.make_async_copy(
                blocks[min(2 * u + half, 12)],
                kv_ref.at[u, :, pl.ds(half * 128, 128)],
                sems.at[2 * u + half],
            ).start()
    w_uv_copy = pltpu.make_async_copy(w_uv_any, w_uv_ref, sems.at[2 * units])
    w_uv_copy.start()
    query_pos = query_base + lax.broadcasted_iota(jnp.int32, (tokens, 1), 0)
    start = jnp.zeros((tokens, 1), jnp.int32)
    first = jnp.int32(0)
    end = jnp.int32(0)
    for k in range(8):
        end = end + lengths_ref[k]
        start = jnp.where(query_pos >= end, end, start)
        first = jnp.where(query_base >= end, end, first)
    lane = lax.broadcasted_iota(jnp.int32, (1, 256), 1)
    scale = 1.0 / math.sqrt(192.0) * math.log2(math.e)

    def base_of(u):
        source = y - u // 2
        source_xh = jnp.where(lax.rem(u, 2) == 0, xh, 1 - xh)
        base = jnp.where(source < 0, 1 << 20, source * 512 + source_xh * 256)
        last = jnp.where((y == 3) & (xh == 0) & (core == 0), 256, 1 << 20)
        return jnp.where(u == units - 1, last, base)

    def seen(u):
        base = base_of(u)
        return (base <= query_base + tokens - 1) & (base + 256 > first)

    def look(u, fresh):
        base, flip = base_of(u), jnp.where(u == units - 1, 0, core)
        key_pos = base + jnp.where(flip > 0, lax.rem(lane + 128, 256), lane)
        visible = (key_pos <= query_pos) & (key_pos >= start)
        s = jnp.dot(qc_ref[...], kv_ref[u, :latent, :], preferred_element_type=jnp.float32)
        s = s + jnp.dot(qr_ref[...], kv_ref[u, latent:, :], preferred_element_type=jnp.float32)
        s = jnp.where(visible[None], s.reshape(heads, tokens, 256), NEVER)
        scores_ref[u] = s.reshape(rows, 256)
        top = jnp.maximum(s[:, :, :128], s[:, :, 128:]).reshape(rows, 128)
        highest_ref[...] = top if fresh else jnp.maximum(highest_ref[...], top)

    def wait(u):
        for half in range(2):
            pltpu.make_async_copy(
                blocks[0], kv_ref.at[u, :, pl.ds(half * 128, 128)], sems.at[2 * u + half]
            ).wait()

    wait(0)
    look(0, True)

    @pl.loop(1, units)
    def _(u):
        wait(u)

        @pl.when(seen(u))
        def _():
            look(u, False)

    highest_ref[:, :1] = jnp.max(highest_ref[...], axis=1, keepdims=True) * scale

    def gather(u, fresh):
        p = jnp.exp2(scores_ref[u] * scale - highest_ref[:, :1])
        product = lax.dot_general(
            p.astype(jnp.bfloat16),
            kv_ref[u, :latent, :],
            (((1,), (1,)), ((), ())),
            preferred_element_type=jnp.float32,
        )
        both = p[:, :128] + p[:, 128:]
        accum_ref[...] = product if fresh else accum_ref[...] + product
        total_ref[...] = both if fresh else total_ref[...] + both

    gather(0, True)

    @pl.loop(1, units)
    def _(u):
        @pl.when(seen(u))
        def _():
            gather(u, False)

    w_uv_copy.wait()
    inverse = 1.0 / jnp.sum(total_ref[...], axis=1, keepdims=True)
    for h in range(heads):
        context = (
            accum_ref[h * tokens : (h + 1) * tokens, :] * inverse[h * tokens : (h + 1) * tokens]
        ).astype(jnp.bfloat16)
        out_ref[:, h * 128 : (h + 1) * 128] = jnp.dot(
            context, w_uv_ref[h], preferred_element_type=jnp.float32
        ).astype(jnp.bfloat16)


def project_kernel(*rest):
    sources = rest[:16]
    own_ref, up_ref, down_ref, far_up_ref, far_down_ref, up2_ref, down2_ref = rest[16:23]
    x_ref, w_ref, sems = rest[23:]
    y, xh, core, z, xl = place_here()
    b, d = z // 2, lax.rem(z, 2)

    def x_copy(number):
        part, g = number // 4, number % 4
        at = pl.multiple_of(lax.rem(y - g - b + 8, 4) * 128, 128)
        return pltpu.make_async_copy(
            sources[number],
            x_ref.at[pl.ds(at, 128), pl.ds(part * 1024, 1024)],
            sems.at[number],
        )

    def w_copy(source, order, part):
        return pltpu.make_async_copy(
            source,
            w_ref.at[order, :, pl.ds(part * 1024, 1024)],
            sems.at[8 + 2 * order + part],
        )

    near_order, far_order = lax.rem(xh + d, 2), lax.rem(1 - xh + d, 2)
    kinds = ((near_order, 0), (near_order, 1), (far_order, 1), (far_order, 0))
    for turn in range(2):

        @pl.when(lax.rem(core + xl, 2) == turn)
        def fetch(turn=turn):
            for kind, (order, part) in enumerate(kinds):
                w_copy(sources[8 + 4 * turn + kind], order, part).start()

    for number in range(8):
        x_copy(number).start()
    for number in range(8):
        x_copy(number).wait()
    pieces = []
    for order in range(2):
        for part in range(2):
            w_copy(sources[8], order, part).wait()
        sums = lax.dot_general(
            w_ref[order], x_ref[...], (((1,), (1,)), ((), ())), preferred_element_type=jnp.float32
        ).astype(jnp.bfloat16)
        parts = [sums[:, j * 128 : (j + 1) * 128] for j in range(4)]
        if order == 0:
            own_ref[...], up2_ref[...] = parts[0], parts[1]
            far_up_ref[...], far_down_ref[...] = parts[2][:224], parts[2][224:]
            down2_ref[...] = parts[3]
        else:
            for turn in range(2):

                @pl.when(d == turn)
                def store(turn=turn):
                    for j in range(4):
                        step = (2 * j + 1 - 2 * turn) % 8
                        ref = up_ref if step < 4 else down_ref
                        ref[0 if step in (3, 5) else 1] = parts[j]


def whole(space):
    return pl.BlockSpec(memory_space=space)


def body(queries, kv_latent, w_uk, w_uv, w_out, doc_lengths):
    rows = queries.shape[0]
    heads, latent, nope = w_uk.shape
    width = w_out.shape[1]

    mine = kv_latent.T

    def from_y(step, flip):
        def target(ty, txh, tcore, tz, txl):
            if ty + step > 3:
                return None
            if flip:
                return (ty + step, 1 - txh, tcore, tz, 1 - txl)
            return (ty + step, txh, tcore, tz, txl)

        return target

    def farthest(ty, txh, tcore, tz, txl):
        if (ty, txh, tcore) == (0, 1, 1):
            return (3, 0, 0, tz, 1 - txl)
        return None

    got = [mine, send(mine, from_y(0, True))]
    for step in (1, 2):
        got.extend([send(mine, from_y(step, False)), send(mine, from_y(step, True))])
    far = send(mine, farthest)
    qc, qr = pl.pallas_call(
        absorb_kernel,
        out_shape=(
            jax.ShapeDtypeStruct((heads * rows, latent), jnp.bfloat16),
            jax.ShapeDtypeStruct((heads * rows, 64), jnp.bfloat16),
        ),
        in_specs=[whole(VMEM), whole(VMEM)],
        out_specs=(whole(VMEM), whole(VMEM)),
        compiler_params=pltpu.CompilerParams(vmem_limit_bytes=8 << 20),
        name="absorb",
    )(queries, w_uk)

    blocks = []
    for block in got[:4]:
        blocks.extend([block, send(block, other_core)])
    for block in after(got[4:], (qc, qr)):
        blocks.extend([block, send(block, other_core)])
    blocks.append(far)
    units = len(got) + 1

    def only(test, goal):
        return lambda *at: goal(*at) if test(*at) else None

    def same(ty, h, c, tz, x):
        return c == x

    def differs(ty, h, c, tz, x):
        return c != x

    def around(ty, h, c, tz, x):
        return (ty, 1 - h, 1 - c, tz, x) if c == x else (ty, h, c, tz, 1 - x)

    def across_x(ty, h, c, tz, x):
        return (ty, 1 - h, 1 - c, tz, 1 - x)

    w_own = w_out.T
    w_a = send(w_own, around)
    w_b = send(after(w_own, got), only(differs, across_x))
    w_a_other = send(after(w_a, blocks), other_core)
    w_own_other = send(after(w_own, blocks), only(same, other_core))

    def shifted(step):
        return lambda ty, txh, tcore, tz, txl: ((ty + step) % 4, txh, tcore, tz, txl)

    qc = after(qc, w_a_other)
    values = pl.pallas_call(
        attend_kernel,
        out_shape=jax.ShapeDtypeStruct((rows, heads * 128), jnp.bfloat16),
        in_specs=[whole(SMEM)] + [whole(VMEM)] * 2 + [whole(pl.ANY)] * 14,
        out_specs=whole(VMEM),
        scratch_shapes=[
            pltpu.VMEM((units, latent + 64, 256), jnp.bfloat16),
            pltpu.VMEM((units, heads * rows, 256), jnp.float32),
            pltpu.VMEM((heads * rows, latent), jnp.float32),
            pltpu.VMEM((heads * rows, 128), jnp.float32),
            pltpu.VMEM((heads * rows, 128), jnp.float32),
            pltpu.VMEM((heads, latent, 128), jnp.bfloat16),
            pltpu.SemaphoreType.DMA((2 * units + 1,)),
        ],
        compiler_params=pltpu.CompilerParams(vmem_limit_bytes=26 << 20),
        name="attend",
    )(doc_lengths, qc, qr, w_uv, *blocks)

    values = after(values, w_own_other)

    near = [values] + [send(values, shifted(step)) for step in (1, 2, 3)]
    neighbour = send(values, other_lo)
    w_b_other = send(after(w_b, (near, neighbour)), only(differs, other_core))
    w_same = [w_own, w_a, w_b_other, w_a_other]
    w_cross = [w_own_other, w_a_other, w_b, w_a]
    across = [
        neighbour,
        send(neighbour, shifted(1)),
        send(near[2], other_lo),
        send(neighbour, shifted(3)),
    ]

    def result(*shape):
        return jax.ShapeDtypeStruct(shape, jnp.bfloat16)

    own, up, down, far_up, far_down, up2, down2 = pl.pallas_call(
        project_kernel,
        out_shape=[
            result(width, rows),
            result(2, width, rows),
            result(2, width, rows),
            result(width // 2, rows),
            result(width // 2, rows),
            result(width, rows),
            result(width, rows),
        ],
        in_specs=[whole(pl.ANY)] * 16,
        out_specs=[whole(VMEM)] * 7,
        scratch_shapes=[
            pltpu.VMEM((4 * rows, 2048), jnp.bfloat16),
            pltpu.VMEM((2, width, 2048), jnp.bfloat16),
            pltpu.SemaphoreType.DMA((12,)),
        ],
        compiler_params=pltpu.CompilerParams(vmem_limit_bytes=20 << 20),
        name="project",
    )(*near, *across, *w_same, *w_cross)

    def along(step):
        return lambda ty, txh, tcore, tz, txl: (ty, txh, tcore, (tz + step) % 8, txl)

    def wide(value):
        return value.astype(jnp.float32)

    from_low = send(up, along(1))
    from_high = send(down, along(7))
    far_up, far_down = after((far_up, far_down), (up, down))
    from_far_low = send(far_up, along(2))
    from_far_high = send(far_down, along(6))
    up_sum = wide(up2) + wide(from_low[0]) + jnp.pad(wide(from_far_low), ((0, width // 2), (0, 0)))
    down_sum = (
        wide(down2) + wide(from_high[0]) + jnp.pad(wide(from_far_high), ((width // 2, 0), (0, 0)))
    )
    total = wide(own) + wide(from_low[1]) + wide(from_high[1])
    total = total + wide(send(up_sum.astype(jnp.bfloat16), along(2)))
    total = total + wide(send(down_sum.astype(jnp.bfloat16), along(6)))
    total = total.astype(jnp.bfloat16)

    def final(ty, txh, tcore, tz, txl):
        return (tz // 2, txh, tcore, 2 * ty + tz % 2, txl)

    return send(total, final).T


def solution(mesh):
    placed = (
        P("ctx", "head"),
        P("ctx", None),
        P("head", None, None),
        P("head", None, None),
        P("head", "ctx"),
        P(),
    )
    return jax.shard_map(
        body, mesh=mesh, in_specs=placed, out_specs=P("ctx", "head"), check_vma=False
    )
```

```python
import math

import jax
import jax.numpy as jnp
from jax import lax
from jax.experimental import pallas as pl
from jax.experimental.pallas import tpu as pltpu
from jax.sharding import PartitionSpec as P

AXES = ("ctx", "head")
VMEM = pltpu.MemorySpace.VMEM
SMEM = pltpu.MemorySpace.SMEM
NEVER = -1e30


def index_of(y, xh, core, z, xl):
    return ((y * 2 + xh) * 2 + core) * 16 + z * 2 + xl


PLACES = [
    (y, xh, core, z, xl)
    for y in range(4)
    for xh in range(2)
    for core in range(2)
    for z in range(8)
    for xl in range(2)
]


def send(value, target):
    pairs = []
    for place in PLACES:
        goal = target(*place)
        if goal is not None:
            pairs.append((index_of(*place), index_of(*goal)))
    return lax.ppermute(value, AXES, pairs)


def other_core(y, xh, core, z, xl):
    return (y, xh, 1 - core, z, xl)


def other_lo(y, xh, core, z, xl):
    return (y, xh, core, z, 1 - xl)


def after(value, earlier):
    return lax.optimization_barrier((value, earlier))[0]


def absorb_kernel(q_ref, w_uk_ref, qc_ref, qr_ref):
    heads, rows = w_uk_ref.shape[0], q_ref.shape[0]
    for h in range(heads):
        nope = q_ref[:, h * 192 : h * 192 + 128]
        qc_ref[h * rows : (h + 1) * rows, :] = lax.dot_general(
            nope, w_uk_ref[h], (((1,), (1,)), ((), ())), preferred_element_type=jnp.float32
        ).astype(jnp.bfloat16)
        qr_ref[h * rows : (h + 1) * rows, :] = q_ref[:, h * 192 + 128 : (h + 1) * 192]


def place_here():
    ctx, head = lax.axis_index("ctx"), lax.axis_index("head")
    return ctx // 4, lax.rem(ctx // 2, 2), lax.rem(ctx, 2), head // 2, lax.rem(head, 2)


def attend_kernel(lengths_ref, qc_ref, qr_ref, w_uv_any, *rest):
    blocks = rest[:13]
    out_ref, kv_ref, scores_ref, accum_ref, highest_ref, total_ref, w_uv_ref, sems = rest[13:]
    y, xh, core, _, _ = place_here()
    rows, latent = qc_ref.shape
    heads = w_uv_ref.shape[0]
    tokens = rows // heads
    units = kv_ref.shape[0]
    query_base = lax.axis_index("ctx") * tokens
    for u in range(units):
        for half in range(2):
            pltpu.make_async_copy(
                blocks[min(2 * u + half, 12)],
                kv_ref.at[u, :, pl.ds(half * 128, 128)],
                sems.at[2 * u + half],
            ).start()
    w_uv_copy = pltpu.make_async_copy(w_uv_any, w_uv_ref, sems.at[2 * units])
    w_uv_copy.start()
    query_pos = query_base + lax.broadcasted_iota(jnp.int32, (tokens, 1), 0)
    start = jnp.zeros((tokens, 1), jnp.int32)
    first = jnp.int32(0)
    end = jnp.int32(0)
    for k in range(8):
        end = end + lengths_ref[k]
        start = jnp.where(query_pos >= end, end, start)
        first = jnp.where(query_base >= end, end, first)
    lane = lax.broadcasted_iota(jnp.int32, (1, 256), 1)
    scale = 1.0 / math.sqrt(192.0) * math.log2(math.e)

    def base_of(u):
        source = y - u // 2
        source_xh = jnp.where(lax.rem(u, 2) == 0, xh, 1 - xh)
        base = jnp.where(source < 0, 1 << 20, source * 512 + source_xh * 256)
        last = jnp.where((y == 3) & (xh == 0) & (core == 0), 256, 1 << 20)
        return jnp.where(u == units - 1, last, base)

    def seen(u):
        base = base_of(u)
        return (base <= query_base + tokens - 1) & (base + 256 > first)

    def look(u, fresh):
        base, flip = base_of(u), jnp.where(u == units - 1, 0, core)
        key_pos = base + jnp.where(flip > 0, lax.rem(lane + 128, 256), lane)
        visible = (key_pos <= query_pos) & (key_pos >= start)
        s = jnp.dot(qc_ref[...], kv_ref[u, :latent, :], preferred_element_type=jnp.float32)
        s = s + jnp.dot(qr_ref[...], kv_ref[u, latent:, :], preferred_element_type=jnp.float32)
        s = jnp.where(visible[None], s.reshape(heads, tokens, 256), NEVER)
        scores_ref[u] = s.reshape(rows, 256)
        top = jnp.maximum(s[:, :, :128], s[:, :, 128:]).reshape(rows, 128)
        highest_ref[...] = top if fresh else jnp.maximum(highest_ref[...], top)

    def wait(u):
        for half in range(2):
            pltpu.make_async_copy(
                blocks[0], kv_ref.at[u, :, pl.ds(half * 128, 128)], sems.at[2 * u + half]
            ).wait()

    wait(0)
    look(0, True)

    @pl.loop(1, units)
    def _(u):
        wait(u)

        @pl.when(seen(u))
        def _():
            look(u, False)

    highest_ref[:, :1] = jnp.max(highest_ref[...], axis=1, keepdims=True) * scale

    def gather(u, fresh):
        p = jnp.exp2(scores_ref[u] * scale - highest_ref[:, :1])
        product = lax.dot_general(
            p.astype(jnp.bfloat16),
            kv_ref[u, :latent, :],
            (((1,), (1,)), ((), ())),
            preferred_element_type=jnp.float32,
        )
        both = p[:, :128] + p[:, 128:]
        accum_ref[...] = product if fresh else accum_ref[...] + product
        total_ref[...] = both if fresh else total_ref[...] + both

    gather(0, True)

    @pl.loop(1, units)
    def _(u):
        @pl.when(seen(u))
        def _():
            gather(u, False)

    w_uv_copy.wait()
    inverse = 1.0 / jnp.sum(total_ref[...], axis=1, keepdims=True)
    for h in range(heads):
        context = (
            accum_ref[h * tokens : (h + 1) * tokens, :] * inverse[h * tokens : (h + 1) * tokens]
        ).astype(jnp.bfloat16)
        out_ref[:, h * 128 : (h + 1) * 128] = jnp.dot(
            context, w_uv_ref[h], preferred_element_type=jnp.float32
        ).astype(jnp.bfloat16)


def project_kernel(*rest):
    sources = rest[:16]
    own_ref, up_ref, down_ref, far_up_ref, far_down_ref, up2_ref, down2_ref = rest[16:23]
    x_ref, w_ref, sems = rest[23:]
    y, xh, core, z, xl = place_here()
    b, d = z // 2, lax.rem(z, 2)

    def x_copy(number):
        part, g = number // 4, number % 4
        at = pl.multiple_of(lax.rem(y - g - b + 8, 4) * 128, 128)
        return pltpu.make_async_copy(
            sources[number],
            x_ref.at[pl.ds(at, 128), pl.ds(part * 1024, 1024)],
            sems.at[number],
        )

    def w_copy(source, order, part):
        return pltpu.make_async_copy(
            source,
            w_ref.at[order, :, pl.ds(part * 1024, 1024)],
            sems.at[8 + 2 * order + part],
        )

    near_order, far_order = lax.rem(xh + d, 2), lax.rem(1 - xh + d, 2)
    kinds = ((near_order, 0), (near_order, 1), (far_order, 1), (far_order, 0))
    for turn in range(2):

        @pl.when(lax.rem(core + xl, 2) == turn)
        def fetch(turn=turn):
            for kind, (order, part) in enumerate(kinds):
                w_copy(sources[8 + 4 * turn + kind], order, part).start()

    for number in range(8):
        x_copy(number).start()
    for number in range(8):
        x_copy(number).wait()
    pieces = []
    for order in range(2):
        for part in range(2):
            w_copy(sources[8], order, part).wait()
        sums = lax.dot_general(
            w_ref[order], x_ref[...], (((1,), (1,)), ((), ())), preferred_element_type=jnp.float32
        ).astype(jnp.bfloat16)
        parts = [sums[:, j * 128 : (j + 1) * 128] for j in range(4)]
        if order == 0:
            own_ref[...], up2_ref[...] = parts[0], parts[1]
            far_up_ref[...], far_down_ref[...] = parts[2][:224], parts[2][224:]
            down2_ref[...] = parts[3]
        else:
            for turn in range(2):

                @pl.when(d == turn)
                def store(turn=turn):
                    for j in range(4):
                        step = (2 * j + 1 - 2 * turn) % 8
                        ref = up_ref if step < 4 else down_ref
                        ref[0 if step in (3, 5) else 1] = parts[j]


def whole(space):
    return pl.BlockSpec(memory_space=space)


def body(queries, kv_latent, w_uk, w_uv, w_out, doc_lengths):
    rows = queries.shape[0]
    heads, latent, nope = w_uk.shape
    width = w_out.shape[1]

    mine = kv_latent.T

    def from_y(step, flip):
        def target(ty, txh, tcore, tz, txl):
            if ty + step > 3:
                return None
            if flip:
                return (ty + step, 1 - txh, tcore, tz, 1 - txl)
            return (ty + step, txh, tcore, tz, txl)

        return target

    def farthest(ty, txh, tcore, tz, txl):
        if (ty, txh, tcore) == (0, 1, 1):
            return (3, 0, 0, tz, 1 - txl)
        return None

    qc, qr = pl.pallas_call(
        absorb_kernel,
        out_shape=(
            jax.ShapeDtypeStruct((heads * rows, latent), jnp.bfloat16),
            jax.ShapeDtypeStruct((heads * rows, 64), jnp.bfloat16),
        ),
        in_specs=[whole(VMEM), whole(VMEM)],
        out_specs=(whole(VMEM), whole(VMEM)),
        compiler_params=pltpu.CompilerParams(vmem_limit_bytes=8 << 20),
        name="absorb",
    )(queries, w_uk)

    got = [mine, send(after(mine, (qc, qr)), from_y(0, True))]
    for step in (1, 2):
        got.extend([send(mine, from_y(step, False)), send(mine, from_y(step, True))])
    far = send(mine, farthest)
    blocks = []
    for block in got[:4]:
        blocks.extend([block, send(block, other_core)])
    for block in got[4:]:
        blocks.extend([block, send(block, other_core)])
    blocks.append(far)
    units = len(got) + 1

    def only(test, goal):
        return lambda *at: goal(*at) if test(*at) else None

    def same(ty, h, c, tz, x):
        return c == x

    def differs(ty, h, c, tz, x):
        return c != x

    def around(ty, h, c, tz, x):
        return (ty, 1 - h, 1 - c, tz, x) if c == x else (ty, h, c, tz, 1 - x)

    def across_x(ty, h, c, tz, x):
        return (ty, 1 - h, 1 - c, tz, 1 - x)

    w_own = w_out.T
    w_a = send(w_own, around)
    w_b = send(after(w_own, got), only(differs, across_x))
    w_a_other = send(after(w_a, blocks), other_core)
    w_own_other = send(after(w_own, blocks), only(same, other_core))

    def shifted(step):
        return lambda ty, txh, tcore, tz, txl: ((ty + step) % 4, txh, tcore, tz, txl)

    qc = after(qc, w_a_other)
    values = pl.pallas_call(
        attend_kernel,
        out_shape=jax.ShapeDtypeStruct((rows, heads * 128), jnp.bfloat16),
        in_specs=[whole(SMEM)] + [whole(VMEM)] * 2 + [whole(pl.ANY)] * 14,
        out_specs=whole(VMEM),
        scratch_shapes=[
            pltpu.VMEM((units, latent + 64, 256), jnp.bfloat16),
            pltpu.VMEM((units, heads * rows, 256), jnp.float32),
            pltpu.VMEM((heads * rows, latent), jnp.float32),
            pltpu.VMEM((heads * rows, 128), jnp.float32),
            pltpu.VMEM((heads * rows, 128), jnp.float32),
            pltpu.VMEM((heads, latent, 128), jnp.bfloat16),
            pltpu.SemaphoreType.DMA((2 * units + 1,)),
        ],
        compiler_params=pltpu.CompilerParams(vmem_limit_bytes=26 << 20),
        name="attend",
    )(doc_lengths, qc, qr, w_uv, *blocks)

    values = after(values, w_own_other)

    near = [values] + [send(values, shifted(step)) for step in (1, 2, 3)]
    neighbour = send(values, other_lo)
    w_b_other = send(after(w_b, (near, neighbour)), only(differs, other_core))
    w_same = [w_own, w_a, w_b_other, w_a_other]
    w_cross = [w_own_other, w_a_other, w_b, w_a]
    across = [
        neighbour,
        send(neighbour, shifted(1)),
        send(near[2], other_lo),
        send(neighbour, shifted(3)),
    ]

    def result(*shape):
        return jax.ShapeDtypeStruct(shape, jnp.bfloat16)

    own, up, down, far_up, far_down, up2, down2 = pl.pallas_call(
        project_kernel,
        out_shape=[
            result(width, rows),
            result(2, width, rows),
            result(2, width, rows),
            result(width // 2, rows),
            result(width // 2, rows),
            result(width, rows),
            result(width, rows),
        ],
        in_specs=[whole(pl.ANY)] * 16,
        out_specs=[whole(VMEM)] * 7,
        scratch_shapes=[
            pltpu.VMEM((4 * rows, 2048), jnp.bfloat16),
            pltpu.VMEM((2, width, 2048), jnp.bfloat16),
            pltpu.SemaphoreType.DMA((12,)),
        ],
        compiler_params=pltpu.CompilerParams(vmem_limit_bytes=20 << 20),
        name="project",
    )(*near, *across, *w_same, *w_cross)

    def along(step):
        return lambda ty, txh, tcore, tz, txl: (ty, txh, tcore, (tz + step) % 8, txl)

    def wide(value):
        return value.astype(jnp.float32)

    from_low = send(up, along(1))
    from_high = send(down, along(7))
    far_up, far_down = after((far_up, far_down), (up, down))
    from_far_low = send(far_up, along(2))
    from_far_high = send(far_down, along(6))
    up_sum = wide(up2) + wide(from_low[0]) + jnp.pad(wide(from_far_low), ((0, width // 2), (0, 0)))
    down_sum = (
        wide(down2) + wide(from_high[0]) + jnp.pad(wide(from_far_high), ((width // 2, 0), (0, 0)))
    )
    total = wide(own) + wide(from_low[1]) + wide(from_high[1])
    total = total + wide(send(up_sum.astype(jnp.bfloat16), along(2)))
    total = total + wide(send(down_sum.astype(jnp.bfloat16), along(6)))
    total = total.astype(jnp.bfloat16)

    def final(ty, txh, tcore, tz, txl):
        return (tz // 2, txh, tcore, 2 * ty + tz % 2, txl)

    return send(total, final).T


def solution(mesh):
    placed = (
        P("ctx", "head"),
        P("ctx", None),
        P("head", None, None),
        P("head", None, None),
        P("head", "ctx"),
        P(),
    )
    return jax.shard_map(
        body, mesh=mesh, in_specs=placed, out_specs=P("ctx", "head"), check_vma=False
    )
```

```python
import math

import jax
import jax.numpy as jnp
from jax import lax
from jax.experimental import pallas as pl
from jax.experimental.pallas import tpu as pltpu
from jax.sharding import PartitionSpec as P

AXES = ("ctx", "head")
VMEM = pltpu.MemorySpace.VMEM
SMEM = pltpu.MemorySpace.SMEM
NEVER = -1e30


def index_of(y, xh, core, z, xl):
    return ((y * 2 + xh) * 2 + core) * 16 + z * 2 + xl


PLACES = [
    (y, xh, core, z, xl)
    for y in range(4)
    for xh in range(2)
    for core in range(2)
    for z in range(8)
    for xl in range(2)
]


def send(value, target):
    pairs = []
    for place in PLACES:
        goal = target(*place)
        if goal is not None:
            pairs.append((index_of(*place), index_of(*goal)))
    return lax.ppermute(value, AXES, pairs)


def other_core(y, xh, core, z, xl):
    return (y, xh, 1 - core, z, xl)


def other_lo(y, xh, core, z, xl):
    return (y, xh, core, z, 1 - xl)


def after(value, earlier):
    return lax.optimization_barrier((value, earlier))[0]


def absorb_kernel(q_ref, w_uk_ref, qc_ref, qr_ref):
    heads, rows = w_uk_ref.shape[0], q_ref.shape[0]
    for h in range(heads):
        nope = q_ref[:, h * 192 : h * 192 + 128]
        qc_ref[h * rows : (h + 1) * rows, :] = lax.dot_general(
            nope, w_uk_ref[h], (((1,), (1,)), ((), ())), preferred_element_type=jnp.float32
        ).astype(jnp.bfloat16)
        qr_ref[h * rows : (h + 1) * rows, :] = q_ref[:, h * 192 + 128 : (h + 1) * 192]


def place_here():
    ctx, head = lax.axis_index("ctx"), lax.axis_index("head")
    return ctx // 4, lax.rem(ctx // 2, 2), lax.rem(ctx, 2), head // 2, lax.rem(head, 2)


def attend_kernel(lengths_ref, qc_ref, qr_ref, w_uv_any, *rest):
    blocks = rest[:13]
    out_ref, kv_ref, scores_ref, accum_ref, highest_ref, total_ref, w_uv_ref, sems = rest[13:]
    y, xh, core, _, _ = place_here()
    rows, latent = qc_ref.shape
    heads = w_uv_ref.shape[0]
    tokens = rows // heads
    units = kv_ref.shape[0]
    query_base = lax.axis_index("ctx") * tokens
    for u in range(units):
        for half in range(2):
            pltpu.make_async_copy(
                blocks[min(2 * u + half, 12)],
                kv_ref.at[u, :, pl.ds(half * 128, 128)],
                sems.at[2 * u + half],
            ).start()
    w_uv_copy = pltpu.make_async_copy(w_uv_any, w_uv_ref, sems.at[2 * units])
    w_uv_copy.start()
    query_pos = query_base + lax.broadcasted_iota(jnp.int32, (tokens, 1), 0)
    start = jnp.zeros((tokens, 1), jnp.int32)
    first = jnp.int32(0)
    end = jnp.int32(0)
    for k in range(8):
        end = end + lengths_ref[k]
        start = jnp.where(query_pos >= end, end, start)
        first = jnp.where(query_base >= end, end, first)
    lane = lax.broadcasted_iota(jnp.int32, (1, 256), 1)
    scale = 1.0 / math.sqrt(192.0) * math.log2(math.e)

    def base_of(u):
        source = y - u // 2
        source_xh = jnp.where(lax.rem(u, 2) == 0, xh, 1 - xh)
        base = jnp.where(source < 0, 1 << 20, source * 512 + source_xh * 256)
        last = jnp.where((y == 3) & (xh == 0) & (core == 0), 256, 1 << 20)
        return jnp.where(u == units - 1, last, base)

    def seen(u):
        base = base_of(u)
        return (base <= query_base + tokens - 1) & (base + 256 > first)

    def look(u, fresh):
        base, flip = base_of(u), jnp.where(u == units - 1, 0, core)
        key_pos = base + jnp.where(flip > 0, lax.rem(lane + 128, 256), lane)
        visible = (key_pos <= query_pos) & (key_pos >= start)
        s = jnp.dot(qc_ref[...], kv_ref[u, :latent, :], preferred_element_type=jnp.float32)
        s = s + jnp.dot(qr_ref[...], kv_ref[u, latent:, :], preferred_element_type=jnp.float32)
        s = jnp.where(visible[None], s.reshape(heads, tokens, 256), NEVER)
        scores_ref[u] = s.reshape(rows, 256)
        top = jnp.maximum(s[:, :, :128], s[:, :, 128:]).reshape(rows, 128)
        highest_ref[...] = top if fresh else jnp.maximum(highest_ref[...], top)

    def wait(u):
        for half in range(2):
            pltpu.make_async_copy(
                blocks[0], kv_ref.at[u, :, pl.ds(half * 128, 128)], sems.at[2 * u + half]
            ).wait()

    wait(0)
    look(0, True)

    @pl.loop(1, units)
    def _(u):
        wait(u)

        @pl.when(seen(u))
        def _():
            look(u, False)

    highest_ref[:, :1] = jnp.max(highest_ref[...], axis=1, keepdims=True) * scale

    def gather(u, fresh):
        p = jnp.exp2(scores_ref[u] * scale - highest_ref[:, :1])
        product = lax.dot_general(
            p.astype(jnp.bfloat16),
            kv_ref[u, :latent, :],
            (((1,), (1,)), ((), ())),
            preferred_element_type=jnp.float32,
        )
        both = p[:, :128] + p[:, 128:]
        accum_ref[...] = product if fresh else accum_ref[...] + product
        total_ref[...] = both if fresh else total_ref[...] + both

    gather(0, True)

    @pl.loop(1, units)
    def _(u):
        @pl.when(seen(u))
        def _():
            gather(u, False)

    w_uv_copy.wait()
    inverse = 1.0 / jnp.sum(total_ref[...], axis=1, keepdims=True)
    for h in range(heads):
        context = (
            accum_ref[h * tokens : (h + 1) * tokens, :] * inverse[h * tokens : (h + 1) * tokens]
        ).astype(jnp.bfloat16)
        out_ref[:, h * 128 : (h + 1) * 128] = jnp.dot(
            context, w_uv_ref[h], preferred_element_type=jnp.float32
        ).astype(jnp.bfloat16)


def project_kernel(*rest):
    sources = rest[:16]
    own_ref, up_ref, down_ref, far_up_ref, far_down_ref, up2_ref, down2_ref = rest[16:23]
    x_ref, w_ref, sems = rest[23:]
    y, xh, core, z, xl = place_here()
    b, d = z // 2, lax.rem(z, 2)

    def x_copy(number):
        part, g = number // 4, number % 4
        at = pl.multiple_of(lax.rem(y - g - b + 8, 4) * 128, 128)
        return pltpu.make_async_copy(
            sources[number],
            x_ref.at[pl.ds(at, 128), pl.ds(part * 1024, 1024)],
            sems.at[number],
        )

    def w_copy(source, order, part):
        return pltpu.make_async_copy(
            source,
            w_ref.at[order, :, pl.ds(part * 1024, 1024)],
            sems.at[8 + 2 * order + part],
        )

    near_order, far_order = lax.rem(xh + d, 2), lax.rem(1 - xh + d, 2)
    kinds = ((near_order, 0), (near_order, 1), (far_order, 1), (far_order, 0))
    for turn in range(2):

        @pl.when(lax.rem(core + xl, 2) == turn)
        def fetch(turn=turn):
            for kind, (order, part) in enumerate(kinds):
                w_copy(sources[8 + 4 * turn + kind], order, part).start()

    for number in range(8):
        x_copy(number).start()
    for number in range(8):
        x_copy(number).wait()
    pieces = []
    for order in range(2):
        for part in range(2):
            w_copy(sources[8], order, part).wait()
        sums = lax.dot_general(
            w_ref[order], x_ref[...], (((1,), (1,)), ((), ())), preferred_element_type=jnp.float32
        ).astype(jnp.bfloat16)
        parts = [sums[:, j * 128 : (j + 1) * 128] for j in range(4)]
        if order == 0:
            own_ref[...], up2_ref[...] = parts[0], parts[1]
            far_up_ref[...], far_down_ref[...] = parts[2][:224], parts[2][224:]
            down2_ref[...] = parts[3]
        else:
            for turn in range(2):

                @pl.when(d == turn)
                def store(turn=turn):
                    for j in range(4):
                        step = (2 * j + 1 - 2 * turn) % 8
                        ref = up_ref if step < 4 else down_ref
                        ref[0 if step in (3, 5) else 1] = parts[j]


def whole(space):
    return pl.BlockSpec(memory_space=space)


def body(queries, kv_latent, w_uk, w_uv, w_out, doc_lengths):
    rows = queries.shape[0]
    heads, latent, nope = w_uk.shape
    width = w_out.shape[1]

    mine = kv_latent.T

    def from_y(step, flip):
        def target(ty, txh, tcore, tz, txl):
            if ty + step > 3:
                return None
            if flip:
                return (ty + step, 1 - txh, tcore, tz, 1 - txl)
            return (ty + step, txh, tcore, tz, txl)

        return target

    def farthest(ty, txh, tcore, tz, txl):
        if (ty, txh, tcore) == (0, 1, 1):
            return (3, 0, 0, tz, 1 - txl)
        return None

    qc, qr = pl.pallas_call(
        absorb_kernel,
        out_shape=(
            jax.ShapeDtypeStruct((heads * rows, latent), jnp.bfloat16),
            jax.ShapeDtypeStruct((heads * rows, 64), jnp.bfloat16),
        ),
        in_specs=[whole(VMEM), whole(VMEM)],
        out_specs=(whole(VMEM), whole(VMEM)),
        compiler_params=pltpu.CompilerParams(vmem_limit_bytes=8 << 20),
        name="absorb",
    )(queries, w_uk)

    got = [mine, send(after(mine, (qc, qr)), from_y(0, True))]
    for step in (1, 2):
        got.extend([send(mine, from_y(step, False)), send(mine, from_y(step, True))])
    far = send(mine, farthest)
    blocks = []
    for block in got[:4]:
        blocks.extend([block, send(block, other_core)])
    for block in got[4:]:
        blocks.extend([block, send(block, other_core)])
    blocks.append(far)
    units = len(got) + 1

    def only(test, goal):
        return lambda *at: goal(*at) if test(*at) else None

    def same(ty, h, c, tz, x):
        return c == x

    def differs(ty, h, c, tz, x):
        return c != x

    def around(ty, h, c, tz, x):
        return (ty, 1 - h, 1 - c, tz, x) if c == x else (ty, h, c, tz, 1 - x)

    def across_x(ty, h, c, tz, x):
        return (ty, 1 - h, 1 - c, tz, 1 - x)

    w_own = w_out.T
    w_a = send(w_own, around)
    w_b = send(after(w_own, got), only(differs, across_x))
    w_a_other = send(after(w_a, blocks), other_core)
    w_own_other = send(after(w_own, blocks), only(same, other_core))

    def shifted(step):
        return lambda ty, txh, tcore, tz, txl: ((ty + step) % 4, txh, tcore, tz, txl)

    qc = after(qc, w_a_other)
    values = pl.pallas_call(
        attend_kernel,
        out_shape=jax.ShapeDtypeStruct((rows, heads * 128), jnp.bfloat16),
        in_specs=[whole(SMEM)] + [whole(VMEM)] * 2 + [whole(pl.ANY)] * 14,
        out_specs=whole(VMEM),
        scratch_shapes=[
            pltpu.VMEM((units, latent + 64, 256), jnp.bfloat16),
            pltpu.VMEM((units, heads * rows, 256), jnp.float32),
            pltpu.VMEM((heads * rows, latent), jnp.float32),
            pltpu.VMEM((heads * rows, 128), jnp.float32),
            pltpu.VMEM((heads * rows, 128), jnp.float32),
            pltpu.VMEM((heads, latent, 128), jnp.bfloat16),
            pltpu.SemaphoreType.DMA((2 * units + 1,)),
        ],
        compiler_params=pltpu.CompilerParams(vmem_limit_bytes=26 << 20),
        name="attend",
    )(doc_lengths, qc, qr, w_uv, *blocks)

    values = after(values, w_own_other)

    near = [values] + [send(values, shifted(step)) for step in (1, 2, 3)]
    neighbour = send(values, other_lo)
    w_b_other = send(after(w_b, (near, neighbour)), only(differs, other_core))
    w_same = [w_own, w_a, w_b_other, w_a_other]
    w_cross = [w_own_other, w_a_other, w_b, w_a]
    across = [
        neighbour,
        send(neighbour, shifted(1)),
        send(near[2], other_lo),
        send(neighbour, shifted(3)),
    ]

    def result(*shape):
        return jax.ShapeDtypeStruct(shape, jnp.bfloat16)

    own, up, down, far_up, far_down, up2, down2 = pl.pallas_call(
        project_kernel,
        out_shape=[
            result(width, rows),
            result(2, width, rows),
            result(2, width, rows),
            result(width // 2, rows),
            result(width // 2, rows),
            result(width, rows),
            result(width, rows),
        ],
        in_specs=[whole(pl.ANY)] * 16,
        out_specs=[whole(VMEM)] * 7,
        scratch_shapes=[
            pltpu.VMEM((4 * rows, 2048), jnp.bfloat16),
            pltpu.VMEM((2, width, 2048), jnp.bfloat16),
            pltpu.SemaphoreType.DMA((12,)),
        ],
        compiler_params=pltpu.CompilerParams(vmem_limit_bytes=20 << 20),
        name="project",
    )(*near, *across, *w_same, *w_cross)

    def along(step):
        return lambda ty, txh, tcore, tz, txl: (ty, txh, tcore, (tz + step) % 8, txl)

    def wide(value):
        return value.astype(jnp.float32)

    from_low = send(up, along(1))
    from_high = send(down, along(7))
    far_up, far_down = after((far_up, far_down), (up, down))
    from_far_low = send(far_up, along(2))
    from_far_high = send(far_down, along(6))
    up_sum = jnp.concatenate(
        [
            wide(up2[: width // 2]) + wide(from_low[0, : width // 2]) + wide(from_far_low),
            wide(up2[width // 2 :]) + wide(from_low[0, width // 2 :]),
        ]
    )
    down_sum = jnp.concatenate(
        [
            wide(down2[: width // 2]) + wide(from_high[0, : width // 2]),
            wide(down2[width // 2 :]) + wide(from_high[0, width // 2 :]) + wide(from_far_high),
        ]
    )
    from_up = send(up_sum.astype(jnp.bfloat16), along(2))
    from_down = send(down_sum.astype(jnp.bfloat16), along(6))
    total = wide(own) + wide(from_low[1]) + wide(from_high[1]) + wide(from_up) + wide(from_down)
    total = total.astype(jnp.bfloat16)

    def final(ty, txh, tcore, tz, txl):
        return (tz // 2, txh, tcore, 2 * ty + tz % 2, txl)

    return send(total, final).T


def solution(mesh):
    placed = (
        P("ctx", "head"),
        P("ctx", None),
        P("head", None, None),
        P("head", None, None),
        P("head", "ctx"),
        P(),
    )
    return jax.shard_map(
        body, mesh=mesh, in_specs=placed, out_specs=P("ctx", "head"), check_vma=False
    )
```
